32 devices in a mesh: ty: 4 (over x, core), tx: 8 (over z, y).
Axes of the slice: x: 2, y: 2, z: 4, core: 2. Of those that a mesh axis runs over, the one named last changes fastest.
Arguments:
- features: bfloat16 [128, 256, 512], P('ty', 'tx'), may hold values from -6 to 6
- block_reduce: bfloat16 [2, 512, 128], replicated, may hold values from -0.375 to 0.375
- block_spatial: bfloat16 [2, 9, 128, 128], replicated, may hold values from -0.25 to 0.25
- block_expand: bfloat16 [2, 128, 512], replicated, may hold values from -0.5 to 0.5
- mask_first: bfloat16 [9, 512, 256], replicated, may hold values from -0.125 to 0.125
- mask_rest: bfloat16 [3, 9, 256, 256], replicated, may hold values from -0.1875 to 0.1875
- mask_logit: bfloat16 [256], replicated, may hold values from -0.5 to 0.5
- box_reduce: bfloat16 [512, 128], replicated, may hold values from -0.25 to 0.25
- box_hidden: bfloat16 [6272, 1024], replicated, may hold values from -0.109375 to 0.109375
- box_second: bfloat16 [1024, 1024], replicated, may hold values from -0.25 to 0.25
- box_predict: bfloat16 [1024, 5], replicated, may hold values from -0.25 to 0.25
- roi_anchor: int32 [4, 8, 32, 2], P('ty', 'tx'), may hold values from 0 to 18
- roi_dest: int32 [4, 8, 32], P('ty', 'tx'), may hold values from -1 to 7, as said below
- roi_slot: int32 [4, 8, 32], P('ty', 'tx'), may hold values from -1 to 15, as said below
Outputs:
- section_features: bfloat16 [128, 256, 512], P('ty', 'tx')
- mask_logits: float32 [4, 8, 32, 196], P('ty', 'tx')
- box_scores: float32 [4, 8, 32, 5], P('ty', 'tx')
The draws below stay inside these ranges and needn't reach their ends.
Inputs may be any that keep to these rules, and one draw needn't show every extreme that they name: `roi_dest`: -1 marks an unused slot; used slots of a tile come first; in each row of tiles every head column receives exactly 16 ROIs; used slots of one tile with the same value lie a multiple of 8 positions apart. -1 exactly where roi_dest is -1; within one row of tiles no two used slots share both roi_dest and roi_slot.
All inputs are finite; a program needn't handle non-finite values.
Results may differ from the reference program's by a relative error of at most 0.033.
Values may be sent and summed in bfloat16 or wider, within the bound.
A program may use at most 128 MiB of HBM per device.

```python
import jax
import jax.numpy as jnp
from jax import lax

CH = 512
INNER = 128
MASK_CH = 256
BOX_CH = 128
FC = 1024
CROP = 14
ROWS = 32
COLS = 32
HEAD = 16
ROI_MAX = 32
TILES_Y = 4
TILES_X = 8


def assign_lists(key):
    perm_key, pair_key, turn_key = jax.random.split(jax.random.fold_in(key, 7), 3)
    row_keys = jax.random.split(perm_key, TILES_Y)
    order = jax.vmap(lambda row_key: jax.random.permutation(row_key, TILES_X))(row_keys)
    amount = jax.random.randint(pair_key, (TILES_Y, TILES_X // 2), 0, HEAD + 1)
    amount = jnp.where(jnp.arange(TILES_X // 2)[None, :] == 0, HEAD, amount)
    paired = jnp.stack([HEAD + amount, HEAD - amount], axis=2).reshape(TILES_Y, TILES_X)
    counts = jnp.take_along_axis(paired, jnp.argsort(order, axis=1), axis=1)
    starts = jnp.cumsum(counts, axis=1) - counts
    turn = jax.random.randint(turn_key, (TILES_Y, 1, 1), 0, TILES_X)
    lane_index = jnp.arange(ROI_MAX)[None, None, :]
    ranking = starts[:, :, None] + lane_index
    is_live = lane_index < counts[:, :, None]
    destination = jnp.where(is_live, (ranking + turn) % TILES_X, -1)
    head_slot = jnp.where(is_live, ranking // TILES_X, -1)
    return (destination.astype(jnp.int32), head_slot.astype(jnp.int32))


def draw_roi_dest(key, part):
    return assign_lists(key)[0]


def draw_roi_slot(key, part):
    return assign_lists(key)[1]


def with_ends(entries, key, smallest, top_value):
    longest = entries.shape.index(max(entries.shape))
    spots = []
    for shift in (0, 1):
        where = [jax.random.randint(jax.random.fold_in(key, axis), (), 0, length) for axis, length in enumerate(entries.shape)]
        where[longest] = (where[longest] + shift) % entries.shape[longest]
        spots.append(tuple(where))
    return entries.at[spots[0]].set(smallest).at[spots[1]].set(top_value)


def shard_levels(rng, dims, cuts, smallest, high):
    def one(axis_at, parts):
        draws = jax.random.uniform(jax.random.fold_in(jax.random.fold_in(rng, 6), axis_at), (parts,), jnp.float32, smallest / len(cuts), high / len(cuts))
        return jnp.repeat(jnp.exp(draws), dims[axis_at] // parts).reshape((-1,) + (1,) * (len(dims) - axis_at - 1))

    factor_of = one(*cuts[0])
    for cut in cuts[1:]:
        factor_of = factor_of * one(*cut)
    return factor_of


def noise(own_key, shape, scale, limit, cuts=(), held_as=jnp.bfloat16):
    drawn = jax.random.normal(own_key, shape, jnp.float32) * scale
    if len(cuts) > 0:
        drawn = shard_levels(own_key, shape, cuts, -0.22, 0.18) * drawn
    return jnp.clip(drawn, min=-limit, max=limit).astype(held_as)


def setup_inputs(seed: int = 0) -> dict:
    keys = jax.random.split(jax.random.key(seed), 15)
    features = noise(keys[0], (TILES_Y * ROWS, TILES_X * COLS, CH), 1.0, 6.0, ((0, 4), (1, 8)))
    block_reduce = noise(keys[1], (2, CH, INNER), (CH // 2) ** -0.5, 0.375)
    block_spatial = noise(keys[2], (2, 9, INNER, INNER), (9 * INNER // 2) ** -0.5, 0.25)
    block_expand = noise(keys[3], (2, INNER, CH), INNER ** -0.5, 0.5)
    mask_first = noise(keys[4], (9, CH, MASK_CH), (9 * CH // 2) ** -0.5, 0.125)
    mask_rest = noise(keys[5], (3, 9, MASK_CH, MASK_CH), (9 * MASK_CH // 2) ** -0.5, 0.1875)
    mask_logit = noise(keys[6], (MASK_CH,), (MASK_CH // 2) ** -0.5, 0.5)
    box_reduce = noise(keys[7], (CH, BOX_CH), CH ** -0.5, 0.25)
    box_hidden = noise(keys[8], ((CROP // 2) ** 2 * BOX_CH, FC), ((CROP // 2) ** 2 * BOX_CH // 2) ** -0.5, 0.109375)
    box_second = noise(keys[9], (FC, FC), (FC // 2) ** -0.5, 0.25)
    box_predict = noise(keys[10], (FC, 5), (FC // 2) ** -0.5, 0.25)
    roi_anchor = with_ends(jax.random.randint(keys[11], (TILES_Y, TILES_X, ROI_MAX, 2), 0, min(ROWS, COLS) - CROP + 1), jax.random.fold_in(keys[11], 1), 0, min(ROWS, COLS) - CROP).astype(jnp.int32)
    roi_dest = draw_roi_dest(jax.random.fold_in(keys[14], 71), 0)
    roi_slot = draw_roi_slot(jax.random.fold_in(keys[14], 71), 0)
    return {"features": features, "block_reduce": block_reduce, "block_spatial": block_spatial, "block_expand": block_expand, "mask_first": mask_first, "mask_rest": mask_rest, "mask_logit": mask_logit, "box_reduce": box_reduce, "box_hidden": box_hidden, "box_second": box_second, "box_predict": box_predict, "roi_anchor": roi_anchor, "roi_dest": roi_dest, "roi_slot": roi_slot}


def conv_three(padded, weights, out_rows, out_cols):
    lead_shape = padded.shape[:-3]
    rows_in, cols_in, chans = padded.shape[-3:]
    width = ((cols_in + 7) // 8) * 8
    pad_spec = [(0, 0)] * len(lead_shape) + [(0, 0), (0, width - cols_in), (0, 0)]
    flat_rows = jnp.pad(padded, pad_spec).reshape(-1, chans)
    row_total = flat_rows.shape[0]
    flat_rows = jnp.pad(flat_rows, ((0, 2 * width + 2), (0, 0)))
    summed = None
    for offset in range(9):
        start_row = (offset // 3) * width + offset % 3
        window = flat_rows[start_row:start_row + row_total]
        partial_sum = jnp.dot(window, weights[offset], preferred_element_type=jnp.float32)
        summed = partial_sum if summed is None else summed + partial_sum
    summed = summed.reshape(lead_shape + (rows_in, width, weights.shape[-1]))
    return summed[..., :out_rows, :out_cols, :]


def pad_crop(crop_batch):
    return jnp.pad(crop_batch, ((0, 0), (1, 1), (1, 1), (0, 0)))


def mask_stem(crops, mask_first, box_reduce):
    number, crop_side = crops.shape[0], crops.shape[1]
    mask_one = jax.nn.relu(conv_three(pad_crop(crops), mask_first, crop_side, crop_side)).astype(jnp.bfloat16)
    reduced = jnp.dot(crops.reshape(-1, crops.shape[-1]), box_reduce, preferred_element_type=jnp.float32)
    half_side = crop_side // 2
    pooled = reduced.reshape(number, half_side, 2, half_side, 2, -1).mean(axis=(2, 4))
    return mask_one, pooled.astype(jnp.bfloat16).reshape(number, -1)


def finish(mask_one, box_input, mask_rest, mask_logit, box_hidden, box_second, box_predict):
    number, crop_side = mask_one.shape[0], mask_one.shape[1]
    mask_layer = mask_one
    for section_index in range(mask_rest.shape[0]):
        mask_layer = jax.nn.relu(conv_three(pad_crop(mask_layer), mask_rest[section_index], crop_side, crop_side)).astype(jnp.bfloat16)
    logits = jnp.dot(mask_layer.reshape(-1, mask_layer.shape[-1]), mask_logit[:, None], preferred_element_type=jnp.float32)
    logits = logits.reshape(number, crop_side * crop_side)
    box_first = jax.nn.relu(jnp.dot(box_input, box_hidden, preferred_element_type=jnp.float32)).astype(jnp.bfloat16)
    box_next = jax.nn.relu(jnp.dot(box_first, box_second, preferred_element_type=jnp.float32)).astype(jnp.bfloat16)
    scores = jnp.dot(box_next, box_predict, preferred_element_type=jnp.float32)
    return logits, scores


def block_step(feature_map, reduce_w, spatial_w, expand_w):
    map_rows, map_cols, chans = feature_map.shape
    inner_map = jax.nn.relu(jnp.dot(feature_map.reshape(-1, chans), reduce_w, preferred_element_type=jnp.float32))
    inner_map = inner_map.astype(jnp.bfloat16).reshape(map_rows, map_cols, -1)
    padded = jnp.pad(inner_map, ((1, 1), (1, 1), (0, 0)))
    spatial = jax.nn.relu(conv_three(padded, spatial_w, map_rows, map_cols)).astype(jnp.bfloat16)
    branch = jnp.dot(spatial.reshape(-1, spatial.shape[-1]), expand_w, preferred_element_type=jnp.float32)
    return jax.nn.relu(feature_map.astype(jnp.float32) + branch.reshape(map_rows, map_cols, chans)).astype(jnp.bfloat16)


def reference(features, block_reduce, block_spatial, block_expand, mask_first, mask_rest, mask_logit, box_reduce, box_hidden, box_second, box_predict, roi_anchor, roi_dest, roi_slot):
    feature_map = features
    for section_index in range(2):
        feature_map = block_step(feature_map, block_reduce[section_index], block_spatial[section_index], block_expand[section_index])
    tile_grid = feature_map.reshape(TILES_Y, ROWS, TILES_X, COLS, CH).transpose(0, 2, 1, 3, 4)

    def cut_crop(tile, anchor):
        start_list = (anchor[0].astype(jnp.int32), anchor[1].astype(jnp.int32), jnp.zeros((), jnp.int32))
        return lax.dynamic_slice(tile, start_list, (CROP, CROP, CH))

    crops = jax.vmap(jax.vmap(jax.vmap(cut_crop, in_axes=(None, 0))))(tile_grid, roi_anchor)
    place_keys = jnp.where(roi_dest >= 0, roi_dest * HEAD + roi_slot, -1).astype(jnp.int32)

    def row_heads(row_item):
        row_crops, row_keys = row_item
        flattened = row_crops.reshape(TILES_X * ROI_MAX, -1)
        places = jnp.arange(TILES_X * HEAD, dtype=jnp.int32)
        chooser = row_keys.reshape(-1)[None, :] == places[:, None]
        compact = jnp.dot(chooser.astype(jnp.bfloat16), flattened, preferred_element_type=jnp.float32)
        compact = compact.astype(jnp.bfloat16).reshape(TILES_X * HEAD, CROP, CROP, CH)
        mask_one, box_input = mask_stem(compact, mask_first, box_reduce)
        logits, scores = finish(mask_one, box_input, mask_rest, mask_logit, box_hidden, box_second, box_predict)
        spread_back = chooser.astype(jnp.float32).T
        return (jnp.dot(spread_back, logits, precision=lax.Precision.HIGHEST),
                jnp.dot(spread_back, scores, precision=lax.Precision.HIGHEST))

    logits, scores = lax.map(row_heads, (crops, place_keys))
    logits = logits.reshape(TILES_Y, TILES_X, ROI_MAX, CROP * CROP)
    scores = scores.reshape(TILES_Y, TILES_X, ROI_MAX, 5)
    return feature_map, logits, scores
```

```python
import jax
import jax.numpy as jnp
import numpy as np
from jax import lax
from jax.experimental import pallas as pl
from jax.experimental.pallas import tpu as pltpu
from jax.sharding import PartitionSpec as P

CROP = 14
SIDE = 32
WIDE = 48
F32 = jnp.float32
BF16 = jnp.bfloat16

DIRS = ((-1, 0), (1, 0), (0, -1), (0, 1), (-1, -1), (-1, 1), (1, -1), (1, 1))
SLOTS = ((0, 64), (64, 64), (128, 64), (192, 64), (256, 16), (272, 16), (288, 16), (304, 16))
EDGE_ROWS = 320


def pack_matrix():
    chosen = np.zeros((192, SIDE * SIDE), np.float32)
    row = 0
    for cols in ((0, 1), (30, 31)):
        for r in range(SIDE):
            for c in cols:
                chosen[row, r * SIDE + c] = 1
                row += 1
    for at, (rows, cols) in enumerate(
        (((0, 1), (0, 1)), ((0, 1), (30, 31)), ((30, 31), (0, 1)), ((30, 31), (30, 31)))
    ):
        for a, r in enumerate(rows):
            for b, c in enumerate(cols):
                chosen[128 + 16 * at + 2 * a + b, r * SIDE + c] = 1
    return chosen


def side_matrix():
    chosen = np.zeros((37, 16, EDGE_ROWS), np.float32)
    for k in range(37):
        for q in (0, 1, 14, 15):
            right = q < 2
            r = k - 3 if right else k - 2
            b = q if right else q - 14
            if r < -2 or r > 33:
                continue
            if r < 0:
                start = (272 if right else 256) + 2 * (r + 2)
            elif r < SIDE:
                start = (192 if right else 128) + 2 * r
            else:
                start = (304 if right else 288) + 2 * (r - SIDE)
            chosen[k, q, start + b] = 1
    return chosen.reshape(37 * 16, EDGE_ROWS)


def halo_kernel(rows_total, cols_total, feat, pack, edges, packed, send_sem, recv_sem):
    row, col = lax.axis_index("ty"), lax.axis_index("tx")

    def exists(step):
        down, across = step
        there = jnp.bool_(True)
        if down:
            there = (row > 0) if down < 0 else (row < rows_total - 1)
        if across:
            side = (col > 0) if across < 0 else (col < cols_total - 1)
            there = jnp.logical_and(there, side) if down else side
        return there

    def target(step):
        return (row + step[0], col + step[1])

    barrier = pltpu.get_barrier_semaphore()
    count = jnp.int32(0)
    for step in DIRS:
        there = exists(step)
        count = count + there.astype(jnp.int32)

        @pl.when(there)
        def _():
            pl.semaphore_signal(
                barrier, inc=1, device_id=target(step), device_id_type=pl.DeviceIdType.MESH
            )

    packed[...] = jnp.dot(pack[...], feat[...], preferred_element_type=F32).astype(BF16)
    pl.semaphore_wait(barrier, count)

    sources = (
        feat.at[pl.ds(0, 64)],
        feat.at[pl.ds(960, 64)],
        packed.at[pl.ds(0, 64)],
        packed.at[pl.ds(64, 64)],
        packed.at[pl.ds(128, 16)],
        packed.at[pl.ds(144, 16)],
        packed.at[pl.ds(160, 16)],
        packed.at[pl.ds(176, 16)],
    )

    def copy_of(at):
        step = DIRS[at]
        back = DIRS.index((-step[0], -step[1]))
        start, size = SLOTS[back]
        return pltpu.make_async_remote_copy(
            src_ref=sources[at],
            dst_ref=edges.at[pl.ds(start, size)],
            send_sem=send_sem.at[at],
            recv_sem=recv_sem.at[back],
            device_id=target(step),
            device_id_type=pl.DeviceIdType.MESH,
        )

    def arrival_of(at):
        start, size = SLOTS[at]
        slot = edges.at[pl.ds(start, size)]
        return pltpu.make_async_remote_copy(
            src_ref=slot,
            dst_ref=slot,
            send_sem=send_sem.at[at],
            recv_sem=recv_sem.at[at],
            device_id=target(DIRS[at]),
            device_id_type=pl.DeviceIdType.MESH,
        )

    for at, step in enumerate(DIRS):

        @pl.when(exists(step))
        def _():
            copy_of(at).start()

        @pl.when(jnp.logical_not(exists(step)))
        def _():
            start, size = SLOTS[at]
            edges[pl.ds(start, size)] = jnp.zeros((size, edges.shape[1]), BF16)

    for at, step in enumerate(DIRS):

        @pl.when(exists(step))
        def _():
            copy_of(at).wait_send()
            arrival_of(at).wait_recv()


def exchange(features, rows_total, cols_total):
    chans = features.shape[1]
    vmem = pl.BlockSpec(memory_space=pltpu.VMEM)
    return pl.pallas_call(
        lambda *refs: halo_kernel(rows_total, cols_total, *refs),
        out_shape=jax.ShapeDtypeStruct((EDGE_ROWS, chans), BF16),
        in_specs=[vmem, vmem],
        out_specs=vmem,
        scratch_shapes=[
            pltpu.VMEM((192, chans), BF16),
            pltpu.SemaphoreType.DMA((8,)),
            pltpu.SemaphoreType.DMA((8,)),
        ],
        compiler_params=pltpu.CompilerParams(
            collective_id=0, has_side_effects=True, vmem_limit_bytes=16 * 2**20
        ),
    )(features, jnp.asarray(pack_matrix(), BF16))


def dot(left, right):
    return jnp.dot(left, right, preferred_element_type=F32)


def shifted(first, middle, last):
    total = first.shape[0]
    return pltpu.roll(first, 1, 0) + middle + pltpu.roll(last, total - 1, 0)


def conv_rows(rows_of, weight_of):
    lhs = jnp.concatenate([rows_of(i) for i in range(3)], axis=1)
    return [
        dot(lhs, jnp.concatenate([weight_of(3 * i + j) for i in range(3)], axis=0))
        for j in range(3)
    ]


GROUP = 4


def main_kernel(
    rows_total,
    cols_total,
    anchor,
    feat,
    edges,
    side,
    reduce_w,
    spatial_w,
    expand_w,
    first_hbm,
    rest_hbm,
    logit_w,
    box_reduce,
    hidden_hbm,
    second_hbm,
    predict_w,
    out_map,
    out_logits,
    out_scores,
    first_w,
    rest_w,
    hidden_w,
    second_w,
    wide,
    inner,
    wide_next,
    tile,
    variants,
    pooled,
    box_in,
    box_sum,
    crop_a,
    crop_b,
    sems,
):
    copies = [
        pltpu.make_async_copy(source, place, sems.at[at])
        for at, (source, place) in enumerate(
            ((first_hbm, first_w), (rest_hbm, rest_w), (hidden_hbm, hidden_w), (second_hbm, second_w))
        )
    ]
    for copy in copies:
        copy.start()
    chans = feat.shape[1]
    row_at, col_at = lax.axis_index("ty"), lax.axis_index("tx")

    ring = dot(side[...], edges[...]).astype(BF16)
    wide[:, 32:48, :] = ring.reshape(37, 16, chans)
    wide[3:35, 0:32, :] = feat[...].reshape(32, 32, chans)
    wide[0:1, 0:32, :] = jnp.zeros((1, 32, chans), BF16)
    wide[1:3, 0:32, :] = edges[0:64, :].reshape(2, 32, chans)
    wide[35:37, 0:32, :] = edges[64:128, :].reshape(2, 32, chans)

    width = reduce_w.shape[2]
    inner[...] = (
        jnp.maximum(dot(wide[...].reshape(37 * WIDE, chans), reduce_w[0]), 0)
        .astype(BF16)
        .reshape(37, WIDE, width)
    )
    parts = conv_rows(
        lambda i: inner[i : i + 35].reshape(35 * WIDE, width), lambda o: spatial_w[0, o]
    )
    spatial = jnp.maximum(shifted(*parts), 0).astype(BF16)
    grown = jnp.maximum(
        wide[1:36].reshape(35 * WIDE, chans).astype(F32) + dot(spatial, expand_w[0]), 0
    ).astype(BF16)
    wide_next[...] = grown.reshape(35, WIDE, chans)

    k_at = lax.broadcasted_iota(jnp.int32, (35, WIDE, width), 0) + 1
    p_at = lax.broadcasted_iota(jnp.int32, (35, WIDE, width), 1)
    is_left = p_at >= 40
    r_at = jnp.where(is_left, k_at - 2, k_at - 3)
    low_r = jnp.where(row_at == 0, 0, -8)
    high_r = jnp.where(row_at == rows_total - 1, 31, 64)
    left_ok = col_at > 0
    high_c = jnp.where(col_at == cols_total - 1, 31, 64)
    low_p = jnp.where(left_ok, 64, 40)
    keep = (r_at >= low_r) & (r_at <= high_r) & (p_at < low_p)
    keep = keep & (is_left | (p_at <= high_c))
    inner_next = jnp.maximum(dot(grown, reduce_w[1]), 0).reshape(35, WIDE, width)
    inner[0:35] = jnp.where(keep, inner_next, 0.0).astype(BF16)
    parts = conv_rows(
        lambda i: inner[i : i + 33].reshape(33 * WIDE, width), lambda o: spatial_w[1, o]
    )
    spatial = jnp.maximum(shifted(*parts), 0).reshape(33, WIDE, width)
    spatial = spatial[1:33, 0:32].reshape(1024, width).astype(BF16)
    result = jnp.maximum(
        wide_next[2:34, 0:32].reshape(1024, chans).astype(F32) + dot(spatial, expand_w[1]), 0
    ).astype(BF16)
    out_map[...] = result
    tile[1:33] = result.reshape(32, 32, chans)
    tile[0:1] = jnp.zeros((1, 32, chans), BF16)
    tile[33:34] = jnp.zeros((1, 32, chans), BF16)

    reduced = dot(result, box_reduce[...])
    pairs = reduced + pltpu.roll(reduced, 1023, 0)
    quads = (pairs + pltpu.roll(pairs, 1024 - 32, 0)) * 0.25
    pooled[...] = quads.astype(BF16).astype(F32).reshape(32, 32, quads.shape[1])

    copies[0].wait()
    out_chans = first_w.shape[2]

    def first_rows(q, carry):
        cols = []
        for i in range(3):
            lhs = tile[pl.ds(q * 8 + i, 8)].reshape(256, chans)
            before, middle, after = (dot(lhs, first_w[3 * i + j]) for j in range(3))
            before = pltpu.roll(before, 1, 0)
            after = pltpu.roll(after, 255, 0)
            left = middle + after
            cols.append((left, before + left, before + middle))
        for v in range(3):
            below = cols[1][v] + cols[2][v]
            for u, value in ((0, below), (1, cols[0][v] + below), (2, cols[0][v] + cols[1][v])):
                value = jnp.maximum(value, 0).astype(BF16).astype(F32).reshape(8, 32, out_chans)
                for h in range(out_chans // 128):
                    variants[h, 3 * u + v, pl.ds(q * 8, 8), 0:32, :] = value[:, :, 128 * h : 128 * h + 128]
        return carry

    lax.fori_loop(0, 4, first_rows, 0)

    slots = anchor.shape[0] // 2
    for crop in (crop_a, crop_b):
        crop[:, 0:1] = jnp.zeros((slots, 1, 16, out_chans), BF16)
        crop[:, 15:16] = jnp.zeros((slots, 1, 16, out_chans), BF16)
    lane = lax.broadcasted_iota(jnp.int32, (8, 128), 0)

    def cut(n, carry):
        r0 = anchor[2 * n]
        c0 = anchor[2 * n + 1]
        for r in range(CROP):
            u = 0 if r == 0 else (2 if r == CROP - 1 else 1)
            for h in range(out_chans // 128):
                low = jnp.where(
                    lane == 0,
                    variants[h, 3 * u, r0 + r, pl.ds(c0, 8), :],
                    variants[h, 3 * u + 1, r0 + r, pl.ds(c0, 8), :],
                )
                high = jnp.where(
                    lane == 5,
                    variants[h, 3 * u + 2, r0 + r, pl.ds(c0 + 8, 8), :],
                    variants[h, 3 * u + 1, r0 + r, pl.ds(c0 + 8, 8), :],
                )
                high = jnp.where(lane < 6, high, 0.0)
                crop_a[n, r + 1, :, 128 * h : 128 * h + 128] = jnp.concatenate(
                    [low, high], axis=0
                ).astype(BF16)
        for a in range(CROP // 2):
            for b in range(CROP // 2):
                box_in[a * 7 + b, pl.ds(n, 1), :] = pooled[r0 + 2 * a, pl.ds(c0 + 2 * b, 1), :]
        return carry

    lax.fori_loop(0, slots, cut, 0)

    copies[1].wait()
    size = GROUP * CROP * 16
    inside = lax.broadcasted_iota(jnp.int32, (size, out_chans), 0) % 16 < CROP

    def layer(q, k, source):
        parts = conv_rows(
            lambda i: source[pl.ds(q * GROUP, GROUP), i : i + CROP].reshape(size, out_chans),
            lambda o: rest_w[k, o],
        )
        value = jnp.maximum(shifted(*parts), 0)
        return jnp.where(inside, value, 0.0).astype(BF16)

    def group(q, carry):
        shape = (GROUP, CROP, 16, out_chans)
        crop_b[pl.ds(q * GROUP, GROUP), 1 : CROP + 1] = layer(q, 0, crop_a).reshape(shape)
        crop_a[pl.ds(q * GROUP, GROUP), 1 : CROP + 1] = layer(q, 1, crop_b).reshape(shape)
        last = layer(q, 2, crop_a)
        out_logits[q] = lax.dot_general(
            logit_w[...], last, (((1,), (1,)), ((), ())), preferred_element_type=F32
        )
        return carry

    lax.fori_loop(0, slots // GROUP, group, 0)

    copies[2].wait()
    copies[3].wait()
    box_sum[...] = jnp.zeros_like(box_sum)
    depth = 7 * box_in.shape[2]

    def hidden(a, carry):
        lhs = jnp.concatenate([box_in[a * 7 + b].astype(BF16) for b in range(7)], axis=1)
        box_sum[...] += dot(lhs, hidden_w[pl.ds(pl.multiple_of(a * depth, 128), depth), :])
        return carry

    lax.fori_loop(0, 7, hidden, 0)
    box_first = jnp.maximum(box_sum[...], 0).astype(BF16)
    box_next = jnp.maximum(dot(box_first, second_w[...]), 0).astype(BF16)
    out_scores[...] = dot(box_next, predict_w[...])


def on_device(
    rows_total,
    cols_total,
    features,
    block_reduce,
    block_spatial,
    block_expand,
    mask_first,
    mask_rest,
    mask_logit,
    box_reduce,
    box_hidden,
    box_second,
    box_predict,
    roi_anchor,
    roi_dest,
    roi_slot,
):
    chans = features.shape[2]
    slots = roi_anchor.shape[2]
    flat = features.reshape(-1, chans)
    edges = exchange(flat, rows_total, cols_total)
    inner_w = block_reduce.shape[2]
    mask_w = mask_first.shape[2]
    box_w = box_reduce.shape[1]
    hidden = box_hidden.shape[1]
    lanes = GROUP * CROP * 16
    vmem = pl.BlockSpec(memory_space=pltpu.VMEM)
    hbm = pl.BlockSpec(memory_space=pl.ANY)
    smem = pl.BlockSpec(memory_space=pltpu.SMEM)
    result, logits, scores = pl.pallas_call(
        lambda *refs: main_kernel(rows_total, cols_total, *refs),
        out_shape=(
            jax.ShapeDtypeStruct(flat.shape, BF16),
            jax.ShapeDtypeStruct((slots // GROUP, 8, lanes), F32),
            jax.ShapeDtypeStruct((slots, box_predict.shape[1]), F32),
        ),
        in_specs=[smem, vmem, vmem, vmem, vmem, vmem, vmem, hbm, hbm, vmem, vmem, hbm, hbm, vmem],
        out_specs=(vmem, vmem, vmem),
        scratch_shapes=[
            pltpu.VMEM(mask_first.shape, BF16),
            pltpu.VMEM(mask_rest.shape, BF16),
            pltpu.VMEM(box_hidden.shape, BF16),
            pltpu.VMEM(box_second.shape, BF16),
            pltpu.VMEM((37, WIDE, chans), BF16),
            pltpu.VMEM((37, WIDE, inner_w), BF16),
            pltpu.VMEM((35, WIDE, chans), BF16),
            pltpu.VMEM((34, 32, chans), BF16),
            pltpu.VMEM((mask_w // 128, 9, 32, 40, 128), F32),
            pltpu.VMEM((32, 32, box_w), F32),
            pltpu.VMEM((49, slots, box_w), F32),
            pltpu.VMEM((slots, hidden), F32),
            pltpu.VMEM((slots, 16, 16, mask_w), BF16),
            pltpu.VMEM((slots, 16, 16, mask_w), BF16),
            pltpu.SemaphoreType.DMA((4,)),
        ],
        compiler_params=pltpu.CompilerParams(vmem_limit_bytes=62 * 2**20),
    )(
        roi_anchor.reshape(-1),
        flat,
        edges,
        jnp.asarray(side_matrix(), BF16),
        block_reduce,
        block_spatial,
        block_expand,
        mask_first,
        mask_rest,
        jnp.broadcast_to(mask_logit[None], (8, mask_w)),
        box_reduce,
        box_hidden,
        box_second,
        box_predict,
    )
    used = roi_dest[0, 0] >= 0
    logits = logits[:, 0].reshape(slots, CROP, 16)[:, :, :CROP].reshape(slots, CROP * CROP)
    logits = jnp.where(used[:, None], logits, 0.0)
    scores = jnp.where(used[:, None], scores, 0.0)
    return (result.reshape(features.shape), logits[None, None], scores[None, None])


def solution(mesh):
    in_specs = (
        P("ty", "tx", None),
        P(),
        P(),
        P(),
        P(),
        P(),
        P(),
        P(),
        P(),
        P(),
        P(),
        P("ty", "tx", None, None),
        P("ty", "tx", None),
        P("ty", "tx", None),
    )
    out_specs = (P("ty", "tx", None), P("ty", "tx", None, None), P("ty", "tx", None, None))
    rows_total, cols_total = mesh.shape["ty"], mesh.shape["tx"]
    return jax.shard_map(
        lambda *arrays: on_device(rows_total, cols_total, *arrays),
        mesh=mesh,
        in_specs=in_specs,
        out_specs=out_specs,
        check_vma=False,
    )
```

```python
import jax
import jax.numpy as jnp
import numpy as np
from jax import lax
from jax.experimental import pallas as pl
from jax.experimental.pallas import tpu as pltpu
from jax.sharding import PartitionSpec as P

CROP = 14
SIDE = 32
WIDE = 48
F32 = jnp.float32
BF16 = jnp.bfloat16

DIRS = ((-1, 0), (1, 0), (0, -1), (0, 1), (-1, -1), (-1, 1), (1, -1), (1, 1))
SLOTS = ((0, 64), (64, 64), (128, 64), (192, 64), (256, 16), (272, 16), (288, 16), (304, 16))
EDGE_ROWS = 320


def pack_matrix():
    chosen = np.zeros((192, SIDE * SIDE), np.float32)
    row = 0
    for cols in ((0, 1), (30, 31)):
        for r in range(SIDE):
            for c in cols:
                chosen[row, r * SIDE + c] = 1
                row += 1
    for at, (rows, cols) in enumerate(
        (((0, 1), (0, 1)), ((0, 1), (30, 31)), ((30, 31), (0, 1)), ((30, 31), (30, 31)))
    ):
        for a, r in enumerate(rows):
            for b, c in enumerate(cols):
                chosen[128 + 16 * at + 2 * a + b, r * SIDE + c] = 1
    return chosen


def side_matrix():
    chosen = np.zeros((37, 16, EDGE_ROWS), np.float32)
    for k in range(37):
        for q in (0, 1, 14, 15):
            right = q < 2
            r = k - 3 if right else k - 2
            b = q if right else q - 14
            if r < -2 or r > 33:
                continue
            if r < 0:
                start = (272 if right else 256) + 2 * (r + 2)
            elif r < SIDE:
                start = (192 if right else 128) + 2 * r
            else:
                start = (304 if right else 288) + 2 * (r - SIDE)
            chosen[k, q, start + b] = 1
    return chosen.reshape(37 * 16, EDGE_ROWS)


def halo_kernel(
    rows_total, cols_total, feat_hbm, pack_hbm, edges, feat, pack, packed, send_sem, recv_sem, load_sem
):
    row, col = lax.axis_index("ty"), lax.axis_index("tx")

    loads = (
        pltpu.make_async_copy(feat_hbm, feat, load_sem.at[0]),
        pltpu.make_async_copy(pack_hbm, pack, load_sem.at[1]),
    )
    for load in loads:
        load.start()

    def exists(step):
        down, across = step
        there = jnp.bool_(True)
        if down:
            there = (row > 0) if down < 0 else (row < rows_total - 1)
        if across:
            side = (col > 0) if across < 0 else (col < cols_total - 1)
            there = jnp.logical_and(there, side) if down else side
        return there

    def target(step):
        return (row + step[0], col + step[1])

    barrier = pltpu.get_barrier_semaphore()
    count = jnp.int32(0)
    for step in DIRS:
        there = exists(step)
        count = count + there.astype(jnp.int32)

        @pl.when(there)
        def _():
            pl.semaphore_signal(
                barrier, inc=1, device_id=target(step), device_id_type=pl.DeviceIdType.MESH
            )

    for load in loads:
        load.wait()
    packed[...] = jnp.dot(pack[...], feat[...], preferred_element_type=F32).astype(BF16)
    pl.semaphore_wait(barrier, count)

    sources = (
        feat.at[pl.ds(0, 64)],
        feat.at[pl.ds(960, 64)],
        packed.at[pl.ds(0, 64)],
        packed.at[pl.ds(64, 64)],
        packed.at[pl.ds(128, 16)],
        packed.at[pl.ds(144, 16)],
        packed.at[pl.ds(160, 16)],
        packed.at[pl.ds(176, 16)],
    )

    def copy_of(at):
        step = DIRS[at]
        back = DIRS.index((-step[0], -step[1]))
        start, size = SLOTS[back]
        return pltpu.make_async_remote_copy(
            src_ref=sources[at],
            dst_ref=edges.at[pl.ds(start, size)],
            send_sem=send_sem.at[at],
            recv_sem=recv_sem.at[back],
            device_id=target(step),
            device_id_type=pl.DeviceIdType.MESH,
        )

    def arrival_of(at):
        start, size = SLOTS[at]
        slot = edges.at[pl.ds(start, size)]
        return pltpu.make_async_remote_copy(
            src_ref=slot,
            dst_ref=slot,
            send_sem=send_sem.at[at],
            recv_sem=recv_sem.at[at],
            device_id=target(DIRS[at]),
            device_id_type=pl.DeviceIdType.MESH,
        )

    for at, step in enumerate(DIRS):

        @pl.when(exists(step))
        def _():
            copy_of(at).start()

    for at, step in enumerate(DIRS):

        @pl.when(exists(step))
        def _():
            copy_of(at).wait_send()
            arrival_of(at).wait_recv()


def exchange(features, rows_total, cols_total):
    chans = features.shape[1]
    hbm = pl.BlockSpec(memory_space=pl.ANY)
    return pl.pallas_call(
        lambda *refs: halo_kernel(rows_total, cols_total, *refs),
        out_shape=jax.ShapeDtypeStruct((EDGE_ROWS, chans), BF16),
        in_specs=[hbm, hbm],
        out_specs=hbm,
        scratch_shapes=[
            pltpu.VMEM(features.shape, BF16),
            pltpu.VMEM((192, SIDE * SIDE), BF16),
            pltpu.VMEM((192, chans), BF16),
            pltpu.SemaphoreType.DMA((8,)),
            pltpu.SemaphoreType.DMA((8,)),
            pltpu.SemaphoreType.DMA((2,)),
        ],
        compiler_params=pltpu.CompilerParams(
            collective_id=0, has_side_effects=True, vmem_limit_bytes=60 * 2**20
        ),
    )(features, jnp.asarray(pack_matrix(), BF16))


def dot(left, right):
    return jnp.dot(left, right, preferred_element_type=F32)


def shifted(first, middle, last):
    total = first.shape[0]
    return pltpu.roll(first, 1, 0) + middle + pltpu.roll(last, total - 1, 0)


def conv_rows(rows_of, weight_of):
    lhs = jnp.concatenate([rows_of(i) for i in range(3)], axis=1)
    return [
        dot(lhs, jnp.concatenate([weight_of(3 * i + j) for i in range(3)], axis=0))
        for j in range(3)
    ]


GROUP = 8


def main_kernel(
    rows_total,
    cols_total,
    anchor,
    dest,
    dest_row,
    feat_hbm,
    edges_hbm,
    side_hbm,
    reduce_hbm,
    spatial_hbm,
    expand_hbm,
    first_hbm,
    rest_hbm,
    logit_w,
    box_reduce_hbm,
    hidden_hbm,
    second_hbm,
    predict_w,
    out_map,
    out_logits,
    out_scores,
    edges,
    side,
    reduce_w,
    spatial_w,
    expand_w,
    first_w,
    rest_w,
    box_reduce,
    hidden_w,
    second_w,
    wide,
    inner,
    wide_next,
    tile,
    variants,
    pooled,
    box_in,
    box_sum,
    mixed_w,
    crop_a,
    crop_b,
    raw,
    sems,
):
    copies = [
        pltpu.make_async_copy(source, place, sems.at[at])
        for at, (source, place) in enumerate(
            (
                (edges_hbm, edges),
                (side_hbm, side),
                (feat_hbm, wide.at[3:35, 0:32]),
                (reduce_hbm, reduce_w),
                (spatial_hbm, spatial_w),
                (expand_hbm, expand_w),
                (box_reduce_hbm, box_reduce),
                (first_hbm, first_w),
                (rest_hbm, rest_w),
                (hidden_hbm, hidden_w),
                (second_hbm, second_w),
            )
        )
    ]
    for copy in copies:
        copy.start()
    chans = wide.shape[2]
    row_at, col_at = lax.axis_index("ty"), lax.axis_index("tx")
    for copy in copies[:6]:
        copy.wait()

    for (down, across), (start, size) in zip(DIRS, SLOTS):
        gone = jnp.bool_(False)
        if down:
            gone = row_at == (0 if down < 0 else rows_total - 1)
        if across:
            gone = gone | (col_at == (0 if across < 0 else cols_total - 1))

        @pl.when(gone)
        def _():
            edges[start : start + size] = jnp.zeros((size, chans), BF16)

    ring = dot(side[...], edges[...]).astype(BF16)
    wide[:, 32:48, :] = ring.reshape(37, 16, chans)
    wide[0:1, 0:32, :] = jnp.zeros((1, 32, chans), BF16)
    wide[1:3, 0:32, :] = edges[0:64, :].reshape(2, 32, chans)
    wide[35:37, 0:32, :] = edges[64:128, :].reshape(2, 32, chans)

    width = reduce_w.shape[2]
    inner[...] = (
        jnp.maximum(dot(wide[...].reshape(37 * WIDE, chans), reduce_w[0]), 0)
        .astype(BF16)
        .reshape(37, WIDE, width)
    )
    parts = conv_rows(
        lambda i: inner[i : i + 35].reshape(35 * WIDE, width), lambda o: spatial_w[0, o]
    )
    spatial = jnp.maximum(shifted(*parts), 0).astype(BF16)
    grown = jnp.maximum(
        wide[1:36].reshape(35 * WIDE, chans).astype(F32) + dot(spatial, expand_w[0]), 0
    ).astype(BF16)
    wide_next[...] = grown.reshape(35, WIDE, chans)

    k_at = lax.broadcasted_iota(jnp.int32, (35, WIDE, width), 0) + 1
    p_at = lax.broadcasted_iota(jnp.int32, (35, WIDE, width), 1)
    is_left = p_at >= 40
    r_at = jnp.where(is_left, k_at - 2, k_at - 3)
    low_r = jnp.where(row_at == 0, 0, -8)
    high_r = jnp.where(row_at == rows_total - 1, 31, 64)
    left_ok = col_at > 0
    high_c = jnp.where(col_at == cols_total - 1, 31, 64)
    low_p = jnp.where(left_ok, 64, 40)
    keep = (r_at >= low_r) & (r_at <= high_r) & (p_at < low_p)
    keep = keep & (is_left | (p_at <= high_c))
    inner_next = jnp.maximum(dot(grown, reduce_w[1]), 0).reshape(35, WIDE, width)
    inner[0:35] = jnp.where(keep, inner_next, 0.0).astype(BF16)
    parts = conv_rows(
        lambda i: inner[i : i + 33].reshape(33 * WIDE, width), lambda o: spatial_w[1, o]
    )
    spatial = jnp.maximum(shifted(*parts), 0).reshape(33, WIDE, width)
    spatial = spatial[1:33, 0:32].reshape(1024, width).astype(BF16)
    result = jnp.maximum(
        wide_next[2:34, 0:32].reshape(1024, chans).astype(F32) + dot(spatial, expand_w[1]), 0
    ).astype(BF16)
    out_map[...] = result
    tile[1:33] = result.reshape(32, 32, chans)
    tile[0:1] = jnp.zeros((1, 32, chans), BF16)
    tile[33:34] = jnp.zeros((1, 32, chans), BF16)

    copies[6].wait()
    reduced = dot(result, box_reduce[...])
    pairs = reduced + pltpu.roll(reduced, 1023, 0)
    quads = (pairs + pltpu.roll(pairs, 1024 - 32, 0)) * 0.25
    pooled[...] = quads.astype(BF16).astype(F32).reshape(32, 32, quads.shape[1])

    copies[7].wait()
    out_chans = first_w.shape[2]

    def first_rows(q, carry):
        cols = []
        for i in range(3):
            lhs = tile[pl.ds(q * 16 + i, 16)].reshape(512, chans)
            before, middle, after = (dot(lhs, first_w[3 * i + j]) for j in range(3))
            before = pltpu.roll(before, 1, 0)
            after = pltpu.roll(after, 511, 0)
            left = middle + after
            cols.append((left, before + left, before + middle))
        for v in range(3):
            below = cols[1][v] + cols[2][v]
            for u, value in ((0, below), (1, cols[0][v] + below), (2, cols[0][v] + cols[1][v])):
                value = jnp.maximum(value, 0).astype(BF16).astype(F32).reshape(16, 32, out_chans)
                for h in range(out_chans // 128):
                    variants[h, 3 * u + v, pl.ds(q * 16, 16), 0:32, :] = value[:, :, 128 * h : 128 * h + 128]
        return carry

    lax.fori_loop(0, 2, first_rows, 0)

    slots = anchor.shape[1]
    for crop in (crop_a, crop_b):
        crop[:, 0, 0] = jnp.zeros((slots, 16, out_chans), BF16)
        crop[:, 1, 7] = jnp.zeros((slots, 16, out_chans), BF16)
    lane = lax.broadcasted_iota(jnp.int32, (8, 128), 0)

    def cut(n, carry):
        r0 = anchor[0, n]
        c0 = anchor[1, n]
        for r in range(CROP):
            u = 0 if r == 0 else (2 if r == CROP - 1 else 1)
            for h in range(out_chans // 128):
                low = jnp.where(
                    lane == 0,
                    variants[h, 3 * u, r0 + r, pl.ds(c0, 8), :],
                    variants[h, 3 * u + 1, r0 + r, pl.ds(c0, 8), :],
                )
                high = jnp.where(
                    lane == 5,
                    variants[h, 3 * u + 2, r0 + r, pl.ds(c0 + 8, 8), :],
                    variants[h, 3 * u + 1, r0 + r, pl.ds(c0 + 8, 8), :],
                )
                high = jnp.where(lane < 6, high, 0.0)
                crop_a[n, (r + 1) % 2, (r + 1) // 2, :, 128 * h : 128 * h + 128] = jnp.concatenate(
                    [low, high], axis=0
                ).astype(BF16)
        for a in range(CROP // 2):
            for b in range(CROP // 2):
                box_in[a * 7 + b, pl.ds(n, 1), :] = pooled[r0 + 2 * a, pl.ds(c0 + 2 * b, 1), :]
        return carry

    lax.fori_loop(0, slots, cut, 0)

    copies[8].wait()

    def mix(at, carry):
        k, j = at // 3, at % 3
        ends = (rest_w[k, j].astype(F32) + rest_w[k, 6 + j].astype(F32)) * 0.5
        centre = rest_w[k, 3 + j].astype(F32) * 0.5
        mixed_w[at, 0] = (ends + centre).astype(BF16)
        mixed_w[at, 1] = (ends - centre).astype(BF16)
        return carry

    lax.fori_loop(0, 9, mix, 0)

    size = GROUP * (CROP // 2) * 16
    inside = lax.broadcasted_iota(jnp.int32, (size, out_chans), 0) % 16 < CROP

    def layer(q, k, source):
        some = pl.ds(q * GROUP, GROUP)
        shape = (size, out_chans)
        d0, d2 = source[some, 0, 0:7].reshape(shape), source[some, 0, 1:8].reshape(shape)
        d1, d3 = source[some, 1, 0:7].reshape(shape), source[some, 1, 1:8].reshape(shape)
        u0, u1, u2, u3 = d0 - d2, d1 + d2, d2 - d1, d1 - d3
        even, odd = [], []
        for j in range(3):
            m0 = dot(u0, rest_w[k, j])
            m1 = dot(u1, mixed_w[3 * k + j, 0])
            m2 = dot(u2, mixed_w[3 * k + j, 1])
            m3 = dot(u3, rest_w[k, 6 + j])
            even.append(m0 + m1 + m2)
            odd.append(m1 - m2 - m3)
        return [
            jnp.where(inside, jnp.maximum(shifted(*parts), 0), 0.0).astype(BF16)
            for parts in (even, odd)
        ]

    def group(q, carry):
        shape = (GROUP, CROP // 2, 16, out_chans)
        some = pl.ds(q * GROUP, GROUP)
        for k, (source, place) in enumerate(((crop_a, crop_b), (crop_b, crop_a))):
            even, odd = layer(q, k, source)
            place[some, 1, 0:7] = even.reshape(shape)
            place[some, 0, 1:8] = odd.reshape(shape)
        each = (CROP // 2) * 16
        query = jnp.broadcast_to(logit_w[...], (8, out_chans))
        for side_at, last in enumerate(layer(q, 2, crop_a)):
            for g in range(GROUP):
                line = lax.dot_general(
                    query,
                    last[g * each : (g + 1) * each],
                    (((1,), (1,)), ((), ())),
                    preferred_element_type=F32,
                )
                used = dest[0, q * GROUP + g] >= 0
                raw[side_at, q * GROUP + g] = jnp.where(used, line, 0.0)
        return carry

    lax.fori_loop(0, slots // GROUP, group, 0)

    each = (CROP // 2) * 16
    a_at = lax.broadcasted_iota(jnp.int32, (each, CROP * CROP), 0)
    b_at = lax.broadcasted_iota(jnp.int32, (each, CROP * CROP), 1)
    t_at, c_at = a_at // 16, a_at % 16
    logits = None
    for side_at in range(2):
        chosen = (b_at == (2 * t_at + side_at) * CROP + c_at) & (c_at < CROP)
        term = jnp.dot(
            raw[side_at, :, 0, :],
            chosen.astype(F32),
            precision=lax.Precision.HIGHEST,
            preferred_element_type=F32,
        )
        logits = term if logits is None else logits + term
    out_logits[...] = logits

    copies[9].wait()
    copies[10].wait()
    box_sum[...] = jnp.zeros_like(box_sum)
    depth = 7 * box_in.shape[2]

    def hidden(a, carry):
        lhs = jnp.concatenate([box_in[a * 7 + b].astype(BF16) for b in range(7)], axis=1)
        box_sum[...] += dot(lhs, hidden_w[pl.ds(pl.multiple_of(a * depth, 128), depth), :])
        return carry

    lax.fori_loop(0, 7, hidden, 0)
    box_first = jnp.maximum(box_sum[...], 0).astype(BF16)
    box_next = jnp.maximum(dot(box_first, second_w[...]), 0).astype(BF16)
    scores = lax.dot_general(
        predict_w[...], box_next, (((1,), (1,)), ((), ())), preferred_element_type=F32
    )
    scores = jnp.where(dest_row[...] >= 0, scores, 0.0)
    out_scores[...] = scores.reshape(out_scores.shape)


def on_device(
    rows_total,
    cols_total,
    features,
    block_reduce,
    block_spatial,
    block_expand,
    mask_first,
    mask_rest,
    mask_logit,
    box_reduce,
    box_hidden,
    box_second,
    box_predict,
    roi_anchor,
    roi_dest,
    roi_slot,
):
    chans = features.shape[2]
    slots = roi_anchor.shape[2]
    flat = features.reshape(-1, chans)
    edges = exchange(flat, rows_total, cols_total)
    inner_w = block_reduce.shape[2]
    mask_w = mask_first.shape[2]
    box_w = box_reduce.shape[1]
    hidden = box_hidden.shape[1]
    outputs = box_predict.shape[1]
    vmem = pl.BlockSpec(memory_space=pltpu.VMEM)
    hbm = pl.BlockSpec(memory_space=pl.ANY)
    smem = pl.BlockSpec(memory_space=pltpu.SMEM)
    side = side_matrix()
    result, logits, scores = pl.pallas_call(
        lambda *refs: main_kernel(rows_total, cols_total, *refs),
        out_shape=(
            jax.ShapeDtypeStruct(flat.shape, BF16),
            jax.ShapeDtypeStruct((slots, CROP * CROP), F32),
            jax.ShapeDtypeStruct((outputs, 1, slots), F32),
        ),
        in_specs=[smem, smem, vmem] + [hbm] * 8 + [vmem] + [hbm] * 3 + [vmem],
        out_specs=(vmem, vmem, vmem),
        scratch_shapes=[
            pltpu.VMEM(edges.shape, BF16),
            pltpu.VMEM(side.shape, BF16),
            pltpu.VMEM(block_reduce.shape, BF16),
            pltpu.VMEM(block_spatial.shape, BF16),
            pltpu.VMEM(block_expand.shape, BF16),
            pltpu.VMEM(mask_first.shape, BF16),
            pltpu.VMEM(mask_rest.shape, BF16),
            pltpu.VMEM(box_reduce.shape, BF16),
            pltpu.VMEM(box_hidden.shape, BF16),
            pltpu.VMEM(box_second.shape, BF16),
            pltpu.VMEM((37, WIDE, chans), BF16),
            pltpu.VMEM((37, WIDE, inner_w), BF16),
            pltpu.VMEM((35, WIDE, chans), BF16),
            pltpu.VMEM((34, 32, chans), BF16),
            pltpu.VMEM((mask_w // 128, 9, 32, 40, 128), F32),
            pltpu.VMEM((32, 32, box_w), F32),
            pltpu.VMEM((49, slots, box_w), F32),
            pltpu.VMEM((slots, hidden), F32),
            pltpu.VMEM((9, 2, mask_w, mask_w), BF16),
            pltpu.VMEM((slots, 2, 8, 16, mask_w), BF16),
            pltpu.VMEM((slots, 2, 8, 16, mask_w), BF16),
            pltpu.VMEM((2, slots, 8, (CROP // 2) * 16), F32),
            pltpu.SemaphoreType.DMA((11,)),
        ],
        compiler_params=pltpu.CompilerParams(vmem_limit_bytes=63 * 2**20),
    )(
        roi_anchor[0, 0].T,
        roi_dest[0],
        roi_dest[0],
        features,
        edges,
        jnp.asarray(side, BF16),
        block_reduce,
        block_spatial,
        block_expand,
        mask_first,
        mask_rest,
        mask_logit[None],
        box_reduce,
        box_hidden,
        box_second,
        box_predict.T,
    )
    scores = scores.transpose(1, 2, 0)[None]
    return (result.reshape(features.shape), logits[None, None], scores)


def solution(mesh):
    in_specs = (
        P("ty", "tx", None),
        P(),
        P(),
        P(),
        P(),
        P(),
        P(),
        P(),
        P(),
        P(),
        P(),
        P("ty", "tx", None, None),
        P("ty", "tx", None),
        P("ty", "tx", None),
    )
    out_specs = (P("ty", "tx", None), P("ty", "tx", None, None), P("ty", "tx", None, None))
    rows_total, cols_total = mesh.shape["ty"], mesh.shape["tx"]
    return jax.shard_map(
        lambda *arrays: on_device(rows_total, cols_total, *arrays),
        mesh=mesh,
        in_specs=in_specs,
        out_specs=out_specs,
        check_vma=False,
    )
```

```python
import jax
import jax.numpy as jnp
import numpy as np
from jax import lax
from jax.experimental import pallas as pl
from jax.experimental.pallas import tpu as pltpu
from jax.sharding import PartitionSpec as P

CROP = 14
SIDE = 32
WIDE = 48
F32 = jnp.float32
BF16 = jnp.bfloat16

DIRS = ((-1, 0), (1, 0), (0, -1), (0, 1), (-1, -1), (-1, 1), (1, -1), (1, 1))
SLOTS = ((0, 64), (64, 64), (128, 64), (192, 64), (256, 16), (272, 16), (288, 16), (304, 16))
EDGE_ROWS = 320


def pack_matrix():
    chosen = np.zeros((192, SIDE * SIDE), np.float32)
    row = 0
    for cols in ((0, 1), (30, 31)):
        for r in range(SIDE):
            for c in cols:
                chosen[row, r * SIDE + c] = 1
                row += 1
    for at, (rows, cols) in enumerate(
        (((0, 1), (0, 1)), ((0, 1), (30, 31)), ((30, 31), (0, 1)), ((30, 31), (30, 31)))
    ):
        for a, r in enumerate(rows):
            for b, c in enumerate(cols):
                chosen[128 + 16 * at + 2 * a + b, r * SIDE + c] = 1
    return chosen


def side_matrix():
    chosen = np.zeros((37, 16, EDGE_ROWS), np.float32)
    for k in range(37):
        for q in (0, 1, 14, 15):
            right = q < 2
            r = k - 3 if right else k - 2
            b = q if right else q - 14
            if r < -2 or r > 33:
                continue
            if r < 0:
                start = (272 if right else 256) + 2 * (r + 2)
            elif r < SIDE:
                start = (192 if right else 128) + 2 * r
            else:
                start = (304 if right else 288) + 2 * (r - SIDE)
            chosen[k, q, start + b] = 1
    return chosen.reshape(37 * 16, EDGE_ROWS)


def halo_kernel(
    rows_total, cols_total, feat_hbm, pack_hbm, edges, feat, pack, packed, send_sem, recv_sem, load_sem
):
    row, col = lax.axis_index("ty"), lax.axis_index("tx")

    loads = (
        pltpu.make_async_copy(feat_hbm, feat, load_sem.at[0]),
        pltpu.make_async_copy(pack_hbm, pack, load_sem.at[1]),
    )
    for load in loads:
        load.start()

    def exists(step):
        down, across = step
        there = jnp.bool_(True)
        if down:
            there = (row > 0) if down < 0 else (row < rows_total - 1)
        if across:
            side = (col > 0) if across < 0 else (col < cols_total - 1)
            there = jnp.logical_and(there, side) if down else side
        return there

    def target(step):
        return (row + step[0], col + step[1])

    barrier = pltpu.get_barrier_semaphore()
    count = jnp.int32(0)
    for step in DIRS:
        there = exists(step)
        count = count + there.astype(jnp.int32)

        @pl.when(there)
        def _():
            pl.semaphore_signal(
                barrier, inc=1, device_id=target(step), device_id_type=pl.DeviceIdType.MESH
            )

    for load in loads:
        load.wait()
    packed[...] = jnp.dot(pack[...], feat[...], preferred_element_type=F32).astype(BF16)
    pl.semaphore_wait(barrier, count)

    sources = (
        feat.at[pl.ds(0, 64)],
        feat.at[pl.ds(960, 64)],
        packed.at[pl.ds(0, 64)],
        packed.at[pl.ds(64, 64)],
        packed.at[pl.ds(128, 16)],
        packed.at[pl.ds(144, 16)],
        packed.at[pl.ds(160, 16)],
        packed.at[pl.ds(176, 16)],
    )

    def copy_of(at):
        step = DIRS[at]
        back = DIRS.index((-step[0], -step[1]))
        start, size = SLOTS[back]
        return pltpu.make_async_remote_copy(
            src_ref=sources[at],
            dst_ref=edges.at[pl.ds(start, size)],
            send_sem=send_sem.at[at],
            recv_sem=recv_sem.at[back],
            device_id=target(step),
            device_id_type=pl.DeviceIdType.MESH,
        )

    def arrival_of(at):
        start, size = SLOTS[at]
        slot = edges.at[pl.ds(start, size)]
        return pltpu.make_async_remote_copy(
            src_ref=slot,
            dst_ref=slot,
            send_sem=send_sem.at[at],
            recv_sem=recv_sem.at[at],
            device_id=target(DIRS[at]),
            device_id_type=pl.DeviceIdType.MESH,
        )

    for at, step in enumerate(DIRS):

        @pl.when(exists(step))
        def _():
            copy_of(at).start()

    for at, step in enumerate(DIRS):

        @pl.when(exists(step))
        def _():
            copy_of(at).wait_send()
            arrival_of(at).wait_recv()


def exchange(features, rows_total, cols_total):
    chans = features.shape[1]
    hbm = pl.BlockSpec(memory_space=pl.ANY)
    return pl.pallas_call(
        lambda *refs: halo_kernel(rows_total, cols_total, *refs),
        out_shape=jax.ShapeDtypeStruct((EDGE_ROWS, chans), BF16),
        in_specs=[hbm, hbm],
        out_specs=hbm,
        scratch_shapes=[
            pltpu.VMEM(features.shape, BF16),
            pltpu.VMEM((192, SIDE * SIDE), BF16),
            pltpu.VMEM((192, chans), BF16),
            pltpu.SemaphoreType.DMA((8,)),
            pltpu.SemaphoreType.DMA((8,)),
            pltpu.SemaphoreType.DMA((2,)),
        ],
        compiler_params=pltpu.CompilerParams(
            collective_id=0, has_side_effects=True, vmem_limit_bytes=60 * 2**20
        ),
    )(features, jnp.asarray(pack_matrix(), BF16))


def dot(left, right):
    return jnp.dot(left, right, preferred_element_type=F32)


def shifted(first, middle, last):
    total = first.shape[0]
    return pltpu.roll(first, 1, 0) + middle + pltpu.roll(last, total - 1, 0)


def conv_rows(rows_of, weight_of):
    lhs = jnp.concatenate([rows_of(i) for i in range(3)], axis=1)
    return [
        dot(lhs, jnp.concatenate([weight_of(3 * i + j) for i in range(3)], axis=0))
        for j in range(3)
    ]


GROUP = 8


def main_kernel(
    rows_total,
    cols_total,
    anchor,
    dest,
    dest_row,
    feat_hbm,
    edges_hbm,
    side_hbm,
    reduce_hbm,
    spatial_hbm,
    expand_hbm,
    first_hbm,
    rest_hbm,
    logit_w,
    box_reduce_hbm,
    hidden_hbm,
    second_hbm,
    predict_w,
    out_map,
    out_logits,
    out_scores,
    edges,
    side,
    reduce_w,
    spatial_w,
    expand_w,
    first_w,
    rest_w,
    box_reduce,
    hidden_w,
    second_w,
    wide,
    inner,
    wide_next,
    tile,
    variants,
    pooled,
    box_in,
    box_sum,
    mixed_w,
    crop_a,
    crop_b,
    raw,
    sems,
):
    copies = [
        pltpu.make_async_copy(source, place, sems.at[at])
        for at, (source, place) in enumerate(
            (
                (edges_hbm, edges),
                (side_hbm, side),
                (feat_hbm, wide.at[3:35, 0:32]),
                (reduce_hbm, reduce_w),
                (spatial_hbm, spatial_w),
                (expand_hbm, expand_w),
                (box_reduce_hbm, box_reduce),
                (first_hbm, first_w),
                (rest_hbm, rest_w),
                (hidden_hbm, hidden_w),
                (second_hbm, second_w),
            )
        )
    ]
    for copy in copies[:7]:
        copy.start()
    chans = wide.shape[2]
    row_at, col_at = lax.axis_index("ty"), lax.axis_index("tx")
    for copy in copies[:6]:
        copy.wait()
    for copy in copies[7:]:
        copy.start()

    for (down, across), (start, size) in zip(DIRS, SLOTS):
        gone = jnp.bool_(False)
        if down:
            gone = row_at == (0 if down < 0 else rows_total - 1)
        if across:
            gone = gone | (col_at == (0 if across < 0 else cols_total - 1))

        @pl.when(gone)
        def _():
            edges[start : start + size] = jnp.zeros((size, chans), BF16)

    ring = dot(side[...], edges[...]).astype(BF16)
    wide[:, 32:48, :] = ring.reshape(37, 16, chans)
    wide[0:1, 0:32, :] = jnp.zeros((1, 32, chans), BF16)
    wide[1:3, 0:32, :] = edges[0:64, :].reshape(2, 32, chans)
    wide[35:37, 0:32, :] = edges[64:128, :].reshape(2, 32, chans)

    width = reduce_w.shape[2]
    inner[...] = (
        jnp.maximum(dot(wide[...].reshape(37 * WIDE, chans), reduce_w[0]), 0)
        .astype(BF16)
        .reshape(37, WIDE, width)
    )
    parts = conv_rows(
        lambda i: inner[i : i + 35].reshape(35 * WIDE, width), lambda o: spatial_w[0, o]
    )
    spatial = jnp.maximum(shifted(*parts), 0).astype(BF16)
    grown = jnp.maximum(
        wide[1:36].reshape(35 * WIDE, chans).astype(F32) + dot(spatial, expand_w[0]), 0
    ).astype(BF16)
    wide_next[...] = grown.reshape(35, WIDE, chans)

    k_at = lax.broadcasted_iota(jnp.int32, (35, WIDE, width), 0) + 1
    p_at = lax.broadcasted_iota(jnp.int32, (35, WIDE, width), 1)
    is_left = p_at >= 40
    r_at = jnp.where(is_left, k_at - 2, k_at - 3)
    low_r = jnp.where(row_at == 0, 0, -8)
    high_r = jnp.where(row_at == rows_total - 1, 31, 64)
    left_ok = col_at > 0
    high_c = jnp.where(col_at == cols_total - 1, 31, 64)
    low_p = jnp.where(left_ok, 64, 40)
    keep = (r_at >= low_r) & (r_at <= high_r) & (p_at < low_p)
    keep = keep & (is_left | (p_at <= high_c))
    inner_next = jnp.maximum(dot(grown, reduce_w[1]), 0).reshape(35, WIDE, width)
    inner[0:35] = jnp.where(keep, inner_next, 0.0).astype(BF16)
    parts = conv_rows(
        lambda i: inner[i : i + 33].reshape(33 * WIDE, width), lambda o: spatial_w[1, o]
    )
    spatial = jnp.maximum(shifted(*parts), 0).reshape(33, WIDE, width)
    spatial = spatial[1:33, 0:32].reshape(1024, width).astype(BF16)
    result = jnp.maximum(
        wide_next[2:34, 0:32].reshape(1024, chans).astype(F32) + dot(spatial, expand_w[1]), 0
    ).astype(BF16)
    out_map[...] = result
    tile[1:33] = result.reshape(32, 32, chans)
    tile[0:1] = jnp.zeros((1, 32, chans), BF16)
    tile[33:34] = jnp.zeros((1, 32, chans), BF16)

    copies[6].wait()
    reduced = dot(result, box_reduce[...])
    pairs = reduced + pltpu.roll(reduced, 1023, 0)
    quads = (pairs + pltpu.roll(pairs, 1024 - 32, 0)) * 0.25
    pooled[...] = quads.astype(BF16).astype(F32).reshape(32, 32, quads.shape[1])

    copies[7].wait()
    out_chans = first_w.shape[2]

    def first_rows(q, carry):
        cols = []
        for i in range(3):
            lhs = tile[pl.ds(q * 16 + i, 16)].reshape(512, chans)
            before, middle, after = (dot(lhs, first_w[3 * i + j]) for j in range(3))
            before = pltpu.roll(before, 1, 0)
            after = pltpu.roll(after, 511, 0)
            left = middle + after
            cols.append((left, before + left, before + middle))
        for v in range(3):
            below = cols[1][v] + cols[2][v]
            for u, value in ((0, below), (1, cols[0][v] + below), (2, cols[0][v] + cols[1][v])):
                value = jnp.maximum(value, 0).astype(BF16).astype(F32).reshape(16, 32, out_chans)
                for h in range(out_chans // 128):
                    variants[h, 3 * u + v, pl.ds(q * 16, 16), 0:32, :] = value[:, :, 128 * h : 128 * h + 128]
        return carry

    lax.fori_loop(0, 2, first_rows, 0)

    slots = anchor.shape[1]
    for crop in (crop_a, crop_b):
        crop[:, 0, 0] = jnp.zeros((GROUP, 16, 3 * out_chans), BF16)
        crop[:, 1, 7] = jnp.zeros((GROUP, 16, 3 * out_chans), BF16)
    lane = lax.broadcasted_iota(jnp.int32, (8, 128), 0)

    def cut(n, g):
        r0 = anchor[0, n]
        c0 = anchor[1, n]
        for r in range(CROP):
            u = 0 if r == 0 else (2 if r == CROP - 1 else 1)
            for h in range(out_chans // 128):
                low = jnp.where(
                    lane == 0,
                    variants[h, 3 * u, r0 + r, pl.ds(c0, 8), :],
                    variants[h, 3 * u + 1, r0 + r, pl.ds(c0, 8), :],
                )
                high = jnp.where(
                    lane == 5,
                    variants[h, 3 * u + 2, r0 + r, pl.ds(c0 + 8, 8), :],
                    variants[h, 3 * u + 1, r0 + r, pl.ds(c0 + 8, 8), :],
                )
                high = jnp.where(lane < 6, high, 0.0)
                cells = jnp.concatenate([low, high], axis=0)
                for at, moved in enumerate((pltpu.roll(cells, 1, 0), cells, pltpu.roll(cells, 15, 0))):
                    first = at * out_chans + 128 * h
                    crop_a[g, (r + 1) % 2, (r + 1) // 2, :, first : first + 128] = moved.astype(BF16)
        for a in range(CROP // 2):
            for b in range(CROP // 2):
                box_in[a * 7 + b, pl.ds(n, 1), :] = pooled[r0 + 2 * a, pl.ds(c0 + 2 * b, 1), :]

    copies[8].wait()

    def mix(at, carry):
        k, j = at // 3, at % 3
        ends = (rest_w[k, j].astype(F32) + rest_w[k, 6 + j].astype(F32)) * 0.5
        centre = rest_w[k, 3 + j].astype(F32) * 0.5
        mixed_w[k, 0, j] = (ends + centre).astype(BF16)
        mixed_w[k, 1, j] = (ends - centre).astype(BF16)
        return carry

    lax.fori_loop(0, 9, mix, 0)

    size = GROUP * (CROP // 2) * 16
    inside = lax.broadcasted_iota(jnp.int32, (size, out_chans), 0) % 16 < CROP

    def layer(k, source):
        depth = 3 * out_chans
        shape, across = (size, depth), (depth, out_chans)
        d0, d2 = source[:, 0, 0:7].reshape(shape), source[:, 0, 1:8].reshape(shape)
        d1, d3 = source[:, 1, 0:7].reshape(shape), source[:, 1, 1:8].reshape(shape)
        m1 = dot(d1 + d2, mixed_w[k, 0].reshape(across))
        m2 = dot(d2 - d1, mixed_w[k, 1].reshape(across))
        even = dot(d0 - d2, rest_w[k, 0:3].reshape(across)) + (m1 + m2)
        odd = (m1 - m2) - dot(d1 - d3, rest_w[k, 6:9].reshape(across))
        return [jnp.where(inside, jnp.maximum(value, 0), 0.0) for value in (even, odd)]

    def spread(value):
        moved = (pltpu.roll(value, 1, 0), value, pltpu.roll(value, size - 1, 0))
        joined = jnp.concatenate([part.astype(BF16) for part in moved], axis=1)
        return joined.reshape(GROUP, CROP // 2, 16, 3 * out_chans)

    def group(q, carry):
        def one(g, inner_carry):
            cut(q * GROUP + g, g)
            return inner_carry

        lax.fori_loop(0, GROUP, one, 0)
        for k, (source, place) in enumerate(((crop_a, crop_b), (crop_b, crop_a))):
            even, odd = layer(k, source)
            place[:, 1, 0:7] = spread(even)
            place[:, 0, 1:8] = spread(odd)
        each = (CROP // 2) * 16
        query = jnp.broadcast_to(logit_w[...].reshape(1, out_chans), (8, out_chans))
        for side_at, last in enumerate(layer(2, crop_a)):
            last = last.astype(BF16)
            for g in range(GROUP):
                line = lax.dot_general(
                    query,
                    last[g * each : (g + 1) * each],
                    (((1,), (1,)), ((), ())),
                    preferred_element_type=F32,
                )
                used = dest[0, q * GROUP + g] >= 0
                raw[side_at, q * GROUP + g] = jnp.where(used, line, 0.0)
        return carry

    lax.fori_loop(0, slots // GROUP, group, 0)

    each = (CROP // 2) * 16
    a_at = lax.broadcasted_iota(jnp.int32, (each, CROP * CROP), 0)
    b_at = lax.broadcasted_iota(jnp.int32, (each, CROP * CROP), 1)
    t_at, c_at = a_at // 16, a_at % 16
    logits = None
    for side_at in range(2):
        chosen = (b_at == (2 * t_at + side_at) * CROP + c_at) & (c_at < CROP)
        term = jnp.dot(
            raw[side_at, :, 0, :],
            chosen.astype(F32),
            precision=lax.Precision.HIGHEST,
            preferred_element_type=F32,
        )
        logits = term if logits is None else logits + term
    out_logits[...] = logits

    copies[9].wait()
    copies[10].wait()
    box_sum[...] = jnp.zeros_like(box_sum)
    depth = 7 * box_in.shape[2]

    def hidden(a, carry):
        lhs = jnp.concatenate([box_in[a * 7 + b].astype(BF16) for b in range(7)], axis=1)
        box_sum[...] += dot(lhs, hidden_w[pl.ds(pl.multiple_of(a * depth, 128), depth), :])
        return carry

    lax.fori_loop(0, 7, hidden, 0)
    box_first = jnp.maximum(box_sum[...], 0).astype(BF16)
    box_next = jnp.maximum(dot(box_first, second_w[...]), 0).astype(BF16)
    scores = lax.dot_general(
        predict_w[...], box_next, (((1,), (1,)), ((), ())), preferred_element_type=F32
    )
    scores = jnp.where(dest_row[...] >= 0, scores, 0.0)
    out_scores[...] = scores.reshape(out_scores.shape)


def on_device(
    rows_total,
    cols_total,
    features,
    block_reduce,
    block_spatial,
    block_expand,
    mask_first,
    mask_rest,
    mask_logit,
    box_reduce,
    box_hidden,
    box_second,
    box_predict,
    roi_anchor,
    roi_dest,
    roi_slot,
):
    chans = features.shape[2]
    slots = roi_anchor.shape[2]
    flat = features.reshape(-1, chans)
    edges = exchange(flat, rows_total, cols_total)
    inner_w = block_reduce.shape[2]
    mask_w = mask_first.shape[2]
    box_w = box_reduce.shape[1]
    hidden = box_hidden.shape[1]
    outputs = box_predict.shape[1]
    vmem = pl.BlockSpec(memory_space=pltpu.VMEM)
    hbm = pl.BlockSpec(memory_space=pl.ANY)
    smem = pl.BlockSpec(memory_space=pltpu.SMEM)
    side = side_matrix()
    result, logits, scores = pl.pallas_call(
        lambda *refs: main_kernel(rows_total, cols_total, *refs),
        out_shape=(
            jax.ShapeDtypeStruct(flat.shape, BF16),
            jax.ShapeDtypeStruct((slots, CROP * CROP), F32),
            jax.ShapeDtypeStruct((outputs, 1, slots), F32),
        ),
        in_specs=[smem, smem, vmem] + [hbm] * 8 + [vmem] + [hbm] * 3 + [vmem],
        out_specs=(vmem, vmem, vmem),
        scratch_shapes=[
            pltpu.VMEM(edges.shape, BF16),
            pltpu.VMEM(side.shape, BF16),
            pltpu.VMEM(block_reduce.shape, BF16),
            pltpu.VMEM(block_spatial.shape, BF16),
            pltpu.VMEM(block_expand.shape, BF16),
            pltpu.VMEM(mask_first.shape, BF16),
            pltpu.VMEM(mask_rest.shape, BF16),
            pltpu.VMEM(box_reduce.shape, BF16),
            pltpu.VMEM(box_hidden.shape, BF16),
            pltpu.VMEM(box_second.shape, BF16),
            pltpu.VMEM((37, WIDE, chans), BF16),
            pltpu.VMEM((37, WIDE, inner_w), BF16),
            pltpu.VMEM((35, WIDE, chans), BF16),
            pltpu.VMEM((34, 32, chans), BF16),
            pltpu.VMEM((mask_w // 128, 9, 32, 40, 128), F32),
            pltpu.VMEM((32, 32, box_w), F32),
            pltpu.VMEM((49, slots, box_w), F32),
            pltpu.VMEM((slots, hidden), F32),
            pltpu.VMEM((3, 2, 3, mask_w, mask_w), BF16),
            pltpu.VMEM((GROUP, 2, 8, 16, 3 * mask_w), BF16),
            pltpu.VMEM((GROUP, 2, 8, 16, 3 * mask_w), BF16),
            pltpu.VMEM((2, slots, 8, (CROP // 2) * 16), F32),
            pltpu.SemaphoreType.DMA((11,)),
        ],
        compiler_params=pltpu.CompilerParams(vmem_limit_bytes=63 * 2**20),
    )(
        roi_anchor[0, 0].T,
        roi_dest[0],
        roi_dest[0],
        features,
        edges,
        jnp.asarray(side, BF16),
        block_reduce,
        block_spatial,
        block_expand,
        mask_first,
        mask_rest,
        mask_logit,
        box_reduce,
        box_hidden,
        box_second,
        box_predict.T,
    )
    scores = scores.transpose(1, 2, 0)[None]
    return (result.reshape(features.shape), logits[None, None], scores)


def solution(mesh):
    in_specs = (
        P("ty", "tx", None),
        P(),
        P(),
        P(),
        P(),
        P(),
        P(),
        P(),
        P(),
        P(),
        P(),
        P("ty", "tx", None, None),
        P("ty", "tx", None),
        P("ty", "tx", None),
    )
    out_specs = (P("ty", "tx", None), P("ty", "tx", None, None), P("ty", "tx", None, None))
    rows_total, cols_total = mesh.shape["ty"], mesh.shape["tx"]
    return jax.shard_map(
        lambda *arrays: on_device(rows_total, cols_total, *arrays),
        mesh=mesh,
        in_specs=in_specs,
        out_specs=out_specs,
        check_vma=False,
    )
```
